32 devices in a mesh: rows: 8 (over z, y), shock: 4 (over x, core).
Axes of the slice: x: 2, y: 2, z: 4, core: 2. Of those that a mesh axis runs over, the one named last changes fastest.
Arguments:
- coefs: bfloat16 [32, 16, 128, 128], P('rows'), may hold values from -0.125 to 0.125
- lag_pattern: int32 [32, 16], replicated, may hold values from 0 to 31, as said below
- loadings: float32 [4096, 128], P('rows'), may hold values from -0.5 to 0.5
- idiosyncratic: float32 [4096], P('rows'), may hold values from 0.5 to 2
- shocked: int32 [512], P('shock'), may hold values from 0 to 4095
Outputs:
- shares: float32 [4096, 512], P('rows', 'shock')
The draws below stay inside these ranges and needn't reach their ends.
Inputs may be any that keep to these rules, and one draw needn't show every extreme that they name: `lag_pattern`: each row holds distinct blocks. The block rows held by any one device along `rows` together read exactly 4 distinct block from the 4 blocks held by every device along `rows`.
All inputs are finite; a program needn't handle non-finite values.
Results may differ from the reference program's by a relative error of at most 0.009.
Values may be sent and summed in bfloat16 or wider, within the bound.
A program may use at most 64 MiB of HBM per device.

```python
import math
import jax
import jax.numpy as jnp
from jax import lax

BSZ = 128
LAGS = 16
FACTORS = 128
BLK_DEV = 4
HORIZONS = 7
BLOCKS = 32
ASSET_COUNT = 4096
SHOCK_COUNT = 512
CAP = 4


def draw_lag_pattern(key, part):
    owners = BLOCKS // BLK_DEV
    total = owners * CAP
    first_key, second_key = jax.random.split(key)
    scores = jax.random.randint(first_key, (owners, owners, BLK_DEV), 0, 1 << 20) * BLK_DEV + jnp.arange(BLK_DEV, dtype=jnp.int32)
    order = jnp.argsort(scores, axis=-1, stable=True)[:, :, :CAP]
    block_ids = (jnp.arange(owners, dtype=jnp.int32)[None, :, None] * BLK_DEV + order).reshape(owners, total)
    mixing = jax.random.randint(second_key, (owners, total), 0, 1 << 20) * total + jnp.arange(total, dtype=jnp.int32)
    shuffle = jnp.argsort(mixing, axis=-1, stable=True)
    block_ids = jnp.take_along_axis(block_ids, shuffle, axis=1)
    slot_pos = jnp.arange(BLK_DEV * LAGS, dtype=jnp.int32) % total
    return block_ids[:, slot_pos].reshape(BLOCKS, LAGS).astype(jnp.int32)


def set_ends(entries, key, low, top_value):
    longest = entries.shape.index(max(entries.shape))
    spots = []
    for shift in (0, 1):
        where = [jax.random.randint(jax.random.fold_in(key, axis), (), 0, length) for axis, length in enumerate(entries.shape)]
        where[longest] = (where[longest] + shift) % entries.shape[longest]
        spots.append(tuple(where))
    return entries.at[spots[0]].set(low).at[spots[1]].set(top_value)


def block_scale(own_key, extent, cuts, least, high):
    def one(dim, shards_of):
        heights = jax.random.uniform(jax.random.fold_in(jax.random.fold_in(own_key, 6), dim), (shards_of,), jnp.float32, least / len(cuts), high / len(cuts))
        return jnp.repeat(jnp.exp(heights), extent[dim] // shards_of).reshape((-1,) + (1,) * (len(extent) - dim - 1))

    gain = one(*cuts[0])
    for cut in cuts[1:]:
        gain = gain * one(*cut)
    return gain


def gaussian(key, shape, width, limit, shards=(), held_as=jnp.bfloat16):
    values = width * jax.random.normal(key, shape, jnp.float32)
    if shards:
        values = values * block_scale(key, shape, shards, -0.22, 0.18)
    return jnp.clip(values, -limit, limit).astype(held_as)


def setup_inputs(seed: int = 0) -> dict:
    splits = jax.random.split(jax.random.key(seed), 6)
    coefs = gaussian(splits[0], (BLOCKS, LAGS, BSZ, BSZ), (LAGS * BSZ) ** -0.5, 0.125, ((0, 8),))
    lag_pattern = draw_lag_pattern(jax.random.fold_in(splits[5], 71), 0)
    loadings = gaussian(splits[2], (ASSET_COUNT, FACTORS), FACTORS ** -0.5, 0.5, ((0, 8),), jnp.float32)
    idiosyncratic = jnp.clip(jnp.exp(math.log(2.0) - 1.3862944 * jax.random.uniform(splits[3], (ASSET_COUNT,), jnp.float32) ** block_scale(splits[3], (ASSET_COUNT,), ((0, 8),), -0.2, 0.2)), 0.5, 2.0)
    shocked = set_ends(jax.random.randint(splits[4], (SHOCK_COUNT,), 0, ASSET_COUNT), jax.random.fold_in(splits[4], 1), 0, ASSET_COUNT - 1).astype(jnp.int32)
    return dict(coefs=coefs, lag_pattern=lag_pattern, loadings=loadings, idiosyncratic=idiosyncratic, shocked=shocked)


def reference(coefs, lag_pattern, loadings, idiosyncratic, shocked):
    picked = loadings[shocked]
    picked_idio = idiosyncratic[shocked]
    scale = jnp.sqrt(lax.optimization_barrier(jnp.sum(picked * picked, axis=1)) + picked_idio)
    assets = loadings.shape[0]
    positions = jnp.arange(assets, dtype=jnp.int32)
    diagonal_hit = (positions[:, None] == shocked[None, :]).astype(jnp.float32)
    impact = jnp.dot(loadings, picked.T, precision=lax.Precision.HIGHEST, preferred_element_type=jnp.float32)
    impact = impact + diagonal_hit * idiosyncratic[:, None]
    impact = impact / scale[None, :]
    present_response = impact.astype(jnp.bfloat16).reshape(BLOCKS, BSZ, SHOCK_COUNT)
    squared_terms = present_response.astype(jnp.float32) ** 2
    for step in range(HORIZONS - 1):

        def one_row(packed, source=present_response):
            row_coef, row_lags = packed
            lagged = source[row_lags].astype(jnp.float32)
            product = jnp.einsum('lij,ljs->is', row_coef.astype(jnp.float32), lagged)
            return product.astype(jnp.bfloat16)
        present_response = lax.map(one_row, (coefs, lag_pattern))
        squared_terms = squared_terms + present_response.astype(jnp.float32) ** 2
    totals = lax.optimization_barrier(jnp.sum(squared_terms, axis=2))
    shares = SHOCK_COUNT * squared_terms / (totals[:, :, None] + 1e-06)
    return shares.reshape(ASSET_COUNT, SHOCK_COUNT)
```

```python
import functools

import jax
import jax.numpy as jnp
from jax import lax
from jax.experimental import pallas as pl
from jax.experimental.pallas import tpu as pltpu
from jax.sharding import PartitionSpec as P

HORIZONS = 7
CHUNKS = 2
HIGHEST = lax.Precision.HIGHEST
MESH = pl.DeviceIdType.MESH


def f32_dot(a, b, dims):
    return lax.dot_general(
        a, b, (dims, ((), ())), precision=HIGHEST, preferred_element_type=jnp.float32
    )


def kernel(
    owners,
    groups,
    capacity,
    relay,
    inv_ref,
    send_ref,
    coefs_ref,
    loadings_ref,
    idio_ref,
    shocked_ref,
    out_ref,
    dense,
    held,
    outgoing,
    parked,
    acc,
    squares,
    pick,
    part,
    parts,
    sums,
    row_sums,
    part_send,
    part_recv,
    sum_send,
    sum_recv,
    send_sem,
    recv_sem,
    fwd_send,
    fwd_recv,
    near_send,
    near_recv,
    tot_send,
    tot_recv,
):
    blk_dev, lags, size, _ = coefs_ref.shape
    local_rows = blk_dev * size
    shocks = shocked_ref.shape[1]
    factors = loadings_ref.shape[1]
    me = lax.axis_index("rows")
    col = lax.axis_index("shock")
    side = lax.rem(me, 2)
    twin = me + 1 - 2 * side
    lines = owners // 2
    line = me // 2

    def along(d):
        return lax.rem(line + d, lines) * 2 + side

    def copy(src, dst, send, recv, row, column):
        return pltpu.make_async_remote_copy(
            src_ref=src,
            dst_ref=dst,
            send_sem=send,
            recv_sem=recv,
            device_id=(row, column),
            device_id_type=MESH,
        )

    order = [d for pair in zip(range(1, lines), range(lines - 1, 0, -1)) for d in pair]
    order = list(dict.fromkeys(order))

    barrier = pltpu.get_barrier_semaphore()
    if relay:
        row_peers = [twin] + [along(d) for d in order]
        for v in row_peers:
            pl.semaphore_signal(barrier, inc=1, device_id=(v, col), device_id_type=MESH)
        n_peers = len(row_peers)
    else:

        def greet(d, _):
            v = lax.rem(me + d, owners)
            pl.semaphore_signal(barrier, inc=1, device_id=(v, col), device_id_type=MESH)
            return 0

        lax.fori_loop(1, owners, greet, 0)
        n_peers = owners - 1
    for d in range(1, groups):
        c = lax.rem(col + d, groups)
        pl.semaphore_signal(barrier, inc=1, device_id=(me, c), device_id_type=MESH)

    ids = lax.broadcasted_iota(jnp.int32, (local_rows, shocks), 0) + me * local_rows
    pick[...] = (ids == shocked_ref[...]).astype(jnp.float32)
    part[0:factors, :] = f32_dot(loadings_ref[...], pick[...], ((0,), (0,)))
    part[factors : factors + 8, :] = f32_dot(idio_ref[...], pick[...], ((1,), (0,)))
    pl.semaphore_wait(barrier, n_peers + groups - 1)

    if relay:
        first = copy(part, parts.at[0], part_send.at[0], part_recv.at[0], twin, col)
        first.start()
    else:

        def send_part(d, _):
            v = lax.rem(me + d, owners)
            copy(part, parts.at[d], part_send.at[d], part_recv.at[d], v, col).start()
            return 0

        lax.fori_loop(1, owners, send_part, 0)

    def place(o, _):
        for r in range(blk_dev):
            for q in range(capacity):
                at = inv_ref[r, o * capacity + q]
                block = coefs_ref[r, jnp.maximum(at, 0)]
                kept = jnp.where(at >= 0, block, jnp.zeros_like(block))
                dense[o, r * size : (r + 1) * size, q * size : (q + 1) * size] = kept
        return 0

    lax.fori_loop(0, owners, place, 0)

    if relay:
        first.wait()
        sums[...] = part[...] + parts[0]
        between = [
            copy(sums, parts.at[d], sum_send.at[d], sum_recv.at[d], along(d), col)
            for d in order
        ]
        for c in between:
            c.start()
        for c in between:
            c.wait()
        found = sums[...]
        for d in order:
            found = found + parts[d]
    else:

        def wait_part(d, _):
            v = lax.rem(me + d, owners)
            copy(part, parts.at[d], part_send.at[d], part_recv.at[d], v, col).wait()
            return 0

        lax.fori_loop(1, owners, wait_part, 0)
        sums[...] = part[...]

        def add_part(d, _):
            sums[...] += parts[d]
            return 0

        lax.fori_loop(1, owners, add_part, 0)
        found = sums[...]
    chosen = found[0:factors]
    chosen_idio = found[factors : factors + 1]
    scale = jnp.sqrt(jnp.sum(chosen * chosen, axis=0, keepdims=True) + chosen_idio)
    impact = f32_dot(loadings_ref[...], chosen, ((1,), (0,)))
    impact = (impact + pick[...] * chosen_idio) / scale
    start = impact.astype(jnp.bfloat16)
    squares[...] = start.astype(jnp.float32) ** 2
    mine = start.reshape(blk_dev, size, shocks)

    def add(p, owner):
        slab = held[p, owner].reshape(capacity * size, shocks)
        acc[...] += jnp.dot(dense[owner], slab, preferred_element_type=jnp.float32)

    rows_of = blk_dev // CHUNKS if relay else 0
    cuts = [pl.ds(c * rows_of, rows_of) for c in range(CHUNKS)] if relay else []

    def relay_step(p):
        sends = []
        for c, cut in enumerate(cuts):
            here = held.at[p, me, cut]
            for d in order:
                k = d * CHUNKS + c
                one = copy(here, here, send_sem.at[k], recv_sem.at[p, k], along(d), col)
                one.start()
                sends.append(one)
            one = copy(here, here, near_send.at[c], near_recv.at[p, c], twin, col)
            one.start()
            sends.append(one)
        acc[...] = jnp.zeros_like(acc)
        add(p, me)
        for d in order:
            src = along(lines - d)
            for c, cut in enumerate(cuts):
                k = d * CHUNKS + c
                there = held.at[p, src, cut]
                copy(there, there, send_sem.at[k], recv_sem.at[p, k], src, col).wait_recv()
                one = copy(there, there, fwd_send.at[k], fwd_recv.at[p, k], twin, col)
                one.start()
                sends.append(one)
            add(p, src)
        for c, cut in enumerate(cuts):
            there = held.at[p, twin, cut]
            copy(there, there, near_send.at[c], near_recv.at[p, c], twin, col).wait_recv()
        add(p, twin)
        for d in order:
            src = lax.rem(line + lines - d, lines) * 2 + 1 - side
            for c, cut in enumerate(cuts):
                k = d * CHUNKS + c
                there = held.at[p, src, cut]
                copy(there, there, fwd_send.at[k], fwd_recv.at[p, k], twin, col).wait_recv()
            add(p, src)
        for one in sends:
            one.wait_send()

    def direct_copy(p, d):
        v = lax.rem(me + d, owners)
        return copy(
            outgoing.at[v], held.at[p, me], send_sem.at[d], recv_sem.at[p, d], v, col
        )

    def direct_step(p):
        def go(d, _):
            direct_copy(p, d).start()
            return 0

        lax.fori_loop(1, owners, go, 0)
        acc[...] = jnp.zeros_like(acc)
        held[p, me] = outgoing[me]
        add(p, me)

        def take(d, _):
            src = lax.rem(me + owners - d, owners)
            there = held.at[p, src]
            copy(there, there, send_sem.at[d], recv_sem.at[p, d], src, col).wait_recv()
            add(p, src)
            return 0

        lax.fori_loop(1, owners, take, 0)

        def sent(d, _):
            direct_copy(p, d).wait_send()
            return 0

        lax.fori_loop(1, owners, sent, 0)

    def stage(p, blocks):
        if relay:
            held[p, me] = blocks
        else:
            parked[...] = blocks

            def fill(v, _):
                for w in range(capacity):
                    outgoing[v, w] = parked[send_ref[v, w]]
                return 0

            lax.fori_loop(0, owners, fill, 0)

    stage(0, mine)

    def horizon(h, _):
        p = lax.rem(h, 2)
        (relay_step if relay else direct_step)(p)
        now = acc[...].astype(jnp.bfloat16)
        squares[...] += now.astype(jnp.float32) ** 2
        stage(1 - p, now.reshape(blk_dev, size, shocks))
        return 0

    lax.fori_loop(0, HORIZONS - 1, horizon, 0)

    ones = jnp.ones((8, shocks), jnp.float32)
    row_sums[0] = f32_dot(ones, squares[...], ((1,), (1,)))
    tots = []
    for d in range(1, groups):
        c = lax.rem(col + d, groups)
        one = copy(row_sums.at[0], row_sums.at[d], tot_send.at[d], tot_recv.at[d], me, c)
        one.start()
        tots.append(one)
    for one in tots:
        one.wait()
    total = row_sums[0]
    for d in range(1, groups):
        total = total + row_sums[d]
    first_row = (lax.broadcasted_iota(jnp.int32, (8, shocks), 0) == 0).astype(jnp.float32)
    spread = f32_dot(total, first_row, ((0,), (0,)))
    out_ref[...] = (shocks * groups) * squares[...] / (spread + 1e-06)


def on_device(coefs, lag_pattern, loadings, idiosyncratic, shocked):
    blk_dev, lags, size, _ = coefs.shape
    owners = lax.axis_size("rows")
    groups = lax.axis_size("shock")
    mine = lax.axis_index("rows")
    capacity = min(blk_dev, max(1, blk_dev * lags // owners))
    relay = capacity == blk_dev and owners % 2 == 0 and blk_dev % CHUNKS == 0
    shocks = shocked.shape[0]
    local_rows = blk_dev * size
    factors = loadings.shape[1]
    n_blocks = owners * blk_dev
    my_lags = lax.dynamic_slice_in_dim(lag_pattern, mine * blk_dev, blk_dev, 0)
    if capacity == blk_dev:
        take = my_lags
        send = jnp.broadcast_to(jnp.arange(blk_dev, dtype=jnp.int32), (owners, blk_dev))
    else:
        ids = jnp.arange(n_blocks, dtype=jnp.int32)
        read = jnp.any(my_lags.reshape(-1, 1) == ids[None, :], axis=0)
        earlier = (ids[:, None] > ids[None, :]) & (
            ids[:, None] // blk_dev == ids[None, :] // blk_dev
        )
        before = jnp.sum(earlier & read[None, :], axis=1, dtype=jnp.int32)
        slot = ids // blk_dev * capacity + before
        hit = my_lags[:, :, None] == ids[None, None, :]
        take = jnp.sum(jnp.where(hit, slot[None, None, :], 0), axis=2)
        reads = lag_pattern.reshape(owners, blk_dev * lags)
        own = mine * blk_dev + jnp.arange(blk_dev, dtype=jnp.int32)
        need = jnp.any(reads[:, :, None] == own[None, None, :], axis=1)
        q = jnp.arange(blk_dev, dtype=jnp.int32)
        ahead = jnp.sum(
            (q[:, None] > q[None, :])[None] & need[:, None, :], axis=2, dtype=jnp.int32
        )
        w = jnp.arange(capacity, dtype=jnp.int32)
        routed = need[:, None, :] & (ahead[:, None, :] == w[None, :, None])
        send = jnp.sum(jnp.where(routed, q[None, None, :], 0), axis=2)
    slots = jnp.arange(owners * capacity, dtype=jnp.int32)
    at = take[:, :, None] == slots[None, None, :]
    lag_ids = jnp.arange(lags, dtype=jnp.int32)[None, :, None]
    inv = jnp.max(jnp.where(at, lag_ids, -1), axis=1)
    idio = jnp.broadcast_to(idiosyncratic[None, :], (8, local_rows))

    vmem = pl.BlockSpec(memory_space=pltpu.VMEM)
    smem = pl.BlockSpec(memory_space=pltpu.SMEM)
    n_sem = owners * CHUNKS
    tall = factors + 8
    dma = pltpu.SemaphoreType.DMA
    n_out = 1 if relay else owners
    return pl.pallas_call(
        functools.partial(kernel, owners, groups, capacity, relay),
        out_shape=jax.ShapeDtypeStruct((local_rows, shocks), jnp.float32),
        in_specs=[smem, smem, vmem, vmem, vmem, vmem],
        out_specs=vmem,
        scratch_shapes=[
            pltpu.VMEM((owners, local_rows, capacity * size), jnp.bfloat16),
            pltpu.VMEM((2, owners, capacity, size, shocks), jnp.bfloat16),
            pltpu.VMEM((n_out, capacity, size, shocks), jnp.bfloat16),
            pltpu.VMEM((blk_dev, size, shocks), jnp.bfloat16),
            pltpu.VMEM((local_rows, shocks), jnp.float32),
            pltpu.VMEM((local_rows, shocks), jnp.float32),
            pltpu.VMEM((local_rows, shocks), jnp.float32),
            pltpu.VMEM((tall, shocks), jnp.float32),
            pltpu.VMEM((owners, tall, shocks), jnp.float32),
            pltpu.VMEM((tall, shocks), jnp.float32),
            pltpu.VMEM((groups, 8, local_rows), jnp.float32),
            dma((owners,)),
            dma((owners,)),
            dma((owners,)),
            dma((owners,)),
            dma((n_sem,)),
            dma((2, n_sem)),
            dma((n_sem,)),
            dma((2, n_sem)),
            dma((CHUNKS,)),
            dma((2, CHUNKS)),
            dma((groups,)),
            dma((groups,)),
        ],
        compiler_params=pltpu.CompilerParams(
            collective_id=0, has_side_effects=True, vmem_limit_bytes=40 * 2**20
        ),
    )(inv, send.astype(jnp.int32), coefs, loadings, idio, shocked[None, :])


def solution(mesh):
    placed = (P("rows", None, None, None), P(), P("rows", None), P("rows"), P("shock"))
    return jax.shard_map(
        on_device, mesh=mesh, in_specs=placed, out_specs=P("rows", "shock"), check_vma=False
    )
```
